256 devices in a mesh: grid: 32 (over z, y), var: 8 (over x, core).
Axes of the slice: x: 4, y: 4, z: 8, core: 2. Of those that a mesh axis runs over, the one named last changes fastest.
Arguments:
- tensor_field: float32 [16, 512, 32768], P('var', None, 'grid'), may hold values from -400 to 400, as said below
- start_basis: float32 [512, 128], replicated, may hold values from -6 to 6
Outputs:
- core_tensor: float32 [16, 128, 32768], P('var', None, 'grid')
- factor_basis: float32 [512, 128], replicated
The draws below stay inside these ranges and needn't reach their ends.
Inputs may be any that keep to these rules, and one draw needn't show every extreme that they name: `tensor_field`: Real-valued field of variables with differing scales.
All inputs are finite; a program needn't handle non-finite values.
Results may differ from the reference program's by a relative error of at most 0.0003.
Values sent between devices are 32-bit elements; how exact they have to be, the bound alone decides.
No kernel may reach another device: no remote copies, remote signals or barrier semaphores. Data moves between devices by JAX's collectives and lax.ppermute only.
A program may use at most 64 MiB of HBM per device.

```python
import jax
import jax.numpy as jnp
from jax import lax

N1 = 512
RANK = 128
COL_DEV = 1024
ITERS = 4
VARS = 16
COLS = 32768


def draw_tensor_field(key, part):
    key = jax.random.fold_in(key, 7)
    keys = jax.random.split(key, 4)
    row_scale = jnp.exp(jax.random.uniform(keys[1], (N1,), jnp.float32, 0.0, 2.302585))
    groups = COLS * 2 // COL_DEV
    block_scale = jnp.exp(jax.random.uniform(keys[2], (N1, groups), jnp.float32, -0.693147, 0.693147))
    block_scale = jnp.repeat(block_scale, COL_DEV // 2, axis=1)
    trend = jnp.sqrt(1.0 + 2.0 * jnp.arange(COLS, dtype=jnp.float32) / COLS)
    var_scale = jnp.exp(jax.random.uniform(keys[3], (VARS,), jnp.float32, -0.693147, 0.693147))
    scale = var_scale[:, None, None] * row_scale[None, :, None] * block_scale[None, :, :] * trend[None, None, :]
    noise = jax.random.truncated_normal(keys[0], -4.0, 4.0, (VARS, N1, COLS), jnp.float32)
    return noise * scale


def centred(stream_key, shape, spread, bound, held_as=jnp.bfloat16):
    result = jax.random.normal(stream_key, shape, jnp.float32) * spread
    return jnp.minimum(jnp.maximum(result, -bound), bound).astype(held_as)


def setup_inputs(seed: int = 0) -> dict:
    seeds = jax.random.split(jax.random.key(seed), 3)
    return {
        "tensor_field": draw_tensor_field(jax.random.fold_in(seeds[2], 71), 0),
        "start_basis": centred(seeds[1], (N1, RANK), 1.0, 6.0, jnp.float32),
    }


def reference(tensor_field, start_basis):
    highest = lax.Precision.HIGHEST
    column_total = tensor_field.shape[0] * tensor_field.shape[2]
    gram_full = lax.dot_general(tensor_field, tensor_field, (((0, 2), (0, 2)), ((), ())), precision=highest) / column_total
    current_basis = start_basis
    for iteration in range(ITERS):
        image_rows = jnp.dot(gram_full, current_basis, precision=highest)
        products = jnp.dot(image_rows.T, image_rows, precision=highest)
        factor = jnp.linalg.cholesky(products)
        current_basis = jax.scipy.linalg.solve_triangular(factor, image_rows.T, lower=True).T
    core_tensor = jnp.einsum('ir,vic->vrc', current_basis, tensor_field, precision=highest)
    return (core_tensor, current_basis)
```

```python
import jax
import jax.numpy as jnp
from jax import lax
from jax.experimental import pallas as pl
from jax.experimental.pallas import tpu as pltpu
from jax.sharding import Mesh, PartitionSpec as P

ITERS = 4
N1 = 512
RANK = 128
PANEL = 16
BLOCK = 128
PAIRS = [(i, j) for i in range(N1 // BLOCK) for j in range(i, N1 // BLOCK)]
HIGHEST = lax.Precision.HIGHEST
STEP = 512


def split(values):
    high = values.astype(jnp.bfloat16)
    low = (values - high.astype(jnp.float32)).astype(jnp.bfloat16)
    return high, low


def dot(left, right, contract):
    return lax.dot_general(left, right, (contract, ((), ())), preferred_element_type=jnp.float32)


def gram_kernel(field_ref, out_ref, total_ref):
    step = pl.program_id(0)
    high, low = split(field_ref[0])
    half = N1 // 2
    nt = ((1,), (1,))

    @pl.when(step == 0)
    def _():
        total_ref[...] = jnp.zeros_like(total_ref)

    total_ref[0] += dot(high[:half], high[:half], nt)
    total_ref[1] += dot(high[half:], high[half:], nt)
    total_ref[2] += dot(high[:half], low[:half], nt)
    total_ref[3] += dot(high[half:], low[half:], nt)
    total_ref[4] += (
        dot(high[:half], high[half:], nt) + dot(high[:half], low[half:], nt) + dot(low[:half], high[half:], nt)
    )

    @pl.when(step == pl.num_programs(0) - 1)
    def _():
        scale = 1.0 / 524288
        top = total_ref[0] + total_ref[2] + total_ref[2].T
        low_corner = total_ref[1] + total_ref[3] + total_ref[3].T
        for index, (i, j) in enumerate(PAIRS):
            if j < 2:
                source = top
            elif i >= 2:
                source = low_corner
            else:
                source = total_ref[4]
            rows = (i % 2) * BLOCK
            columns = (j % 2) * BLOCK
            out_ref[index] = source[rows : rows + BLOCK, columns : columns + BLOCK] * scale


def partial_gram(field):
    variables, _, columns = field.shape
    parts = columns // STEP
    return pl.pallas_call(
        gram_kernel,
        grid=(variables * parts,),
        in_specs=[pl.BlockSpec((1, N1, STEP), lambda s: (s // parts, 0, s % parts))],
        out_specs=pl.BlockSpec((len(PAIRS), BLOCK, BLOCK), lambda s: (0, 0, 0)),
        out_shape=jax.ShapeDtypeStruct((len(PAIRS), BLOCK, BLOCK), jnp.float32),
        scratch_shapes=[pltpu.VMEM((5, N1 // 2, N1 // 2), jnp.float32)],
        compiler_params=pltpu.CompilerParams(vmem_limit_bytes=24 << 20),
    )(field)


def inverse_factor(products):
    panels = RANK // PANEL
    shape = (PANEL, RANK)
    row = lax.broadcasted_iota(jnp.int32, shape, 0)
    lane = lax.broadcasted_iota(jnp.int32, shape, 1)
    rows = [products[PANEL * r : PANEL * (r + 1), :] for r in range(panels)]
    done = []
    for r in range(panels):
        first = PANEL * r
        panel = rows[r]
        columns = [jnp.broadcast_to(panel[:, first + k : first + k + 1], shape) for k in range(PANEL)]
        inside = (lane >= first) & (lane < first + PANEL)
        panel = jnp.where(inside, jnp.where(lane - first == row, 1.0, 0.0), panel)
        scale = jnp.zeros(shape, jnp.float32)
        for k in range(PANEL):
            pivot = jnp.broadcast_to(columns[k][k : k + 1, :], shape)
            scale = jnp.where(row == k, lax.rsqrt(pivot), scale)
            if k < PANEL - 1:
                factor = jnp.where(row > k, columns[k] * (1.0 / pivot), 0.0)
                for j in range(k + 1, PANEL):
                    columns[j] = columns[j] - factor * jnp.broadcast_to(columns[j][k : k + 1, :], shape)
                panel = panel - factor * jnp.broadcast_to(panel[k : k + 1, :], shape)
        panel = panel * scale
        done.append(jnp.where(lane < first + PANEL, panel, 0.0))
        if r == panels - 1:
            break
        after = [jnp.where(inside, 0.0, rows[q]) if q > r else None for q in range(panels)]
        update = jnp.zeros(shape, jnp.float32)
        for i in range(PANEL):
            at = first + PANEL + i
            weights = jnp.broadcast_to(panel[:, at : at + 1], shape)
            total = jnp.sum(weights * panel, axis=0, keepdims=True)
            update = jnp.where(row == i, jnp.broadcast_to(total, shape), update)
        after[r + 1] = after[r + 1] - update
        if r + 2 < panels:
            start = PANEL * (r + 2)
            trail = lax.dot_general(
                panel[:, start:],
                panel,
                (((0,), (0,)), ((), ())),
                precision=HIGHEST,
                preferred_element_type=jnp.float32,
            )
            for q in range(r + 2, panels):
                offset = PANEL * (q - r - 2)
                after[q] = after[q] - trail[offset : offset + PANEL, :]
        rows = after
    return jnp.concatenate(done, axis=0)


def exact_dot(left, right, contract):
    return lax.dot_general(
        left, right, (contract, ((), ())), precision=HIGHEST, preferred_element_type=jnp.float32
    )


def sweeps_kernel(core_ref, own_ref, other_ref, basis_ref, out_ref, gram_ref, image_ref, ahead_ref):
    own_first = core_ref[0] == 0
    rows_half = own_ref.shape[0]
    for index, (i, j) in enumerate(PAIRS):
        at = (index * BLOCK) % rows_half
        own = own_ref[at : at + BLOCK, :]
        other = other_ref[at : at + BLOCK, :]
        in_first = index * BLOCK < rows_half
        block = jnp.where(own_first == in_first, own, other)
        gram_ref[BLOCK * i : BLOCK * (i + 1), BLOCK * j : BLOCK * (j + 1)] = block
        if i != j:
            gram_ref[BLOCK * j : BLOCK * (j + 1), BLOCK * i : BLOCK * (i + 1)] = block.T
    nn = ((1,), (0,))
    image_ref[...] = exact_dot(gram_ref[...], basis_ref[...], nn)

    def sweep(iteration, carry):
        image = image_ref[...]
        products = exact_dot(image, image, ((0,), (0,)))
        ahead_ref[...] = exact_dot(gram_ref[...], image, nn)
        inverse = inverse_factor(products)
        image_ref[...] = exact_dot(ahead_ref[...], inverse, ((1,), (1,)))
        return carry

    lax.fori_loop(0, ITERS - 1, sweep, 0)
    image = image_ref[...]
    products = exact_dot(image, image, ((0,), (0,)))
    inverse = inverse_factor(products)
    out_ref[...] = exact_dot(image, inverse, ((1,), (1,)))


def sweeps(core, own, other, start_basis):
    whole = pl.BlockSpec(memory_space=pltpu.VMEM)
    return pl.pallas_call(
        sweeps_kernel,
        in_specs=[pl.BlockSpec(memory_space=pltpu.SMEM), whole, whole, whole],
        out_specs=whole,
        out_shape=jax.ShapeDtypeStruct((N1, RANK), jnp.float32),
        scratch_shapes=[
            pltpu.VMEM((N1, N1), jnp.float32),
            pltpu.VMEM((N1, RANK), jnp.float32),
            pltpu.VMEM((N1, RANK), jnp.float32),
        ],
        compiler_params=pltpu.CompilerParams(vmem_limit_bytes=24 << 20),
    )(core, own, other, start_basis)


def core_kernel(basis_ref, field_ref, out_ref):
    tn = ((0,), (0,))
    basis_high, basis_low = split(basis_ref[...])
    high, low = split(field_ref[0])
    out_ref[0] = dot(basis_high, high, tn) + dot(basis_high, low, tn) + dot(basis_low, high, tn)


def project(basis, field):
    variables, _, columns = field.shape
    parts = columns // STEP
    return pl.pallas_call(
        core_kernel,
        grid=(variables, parts),
        in_specs=[
            pl.BlockSpec((N1, RANK), lambda v, s: (0, 0)),
            pl.BlockSpec((1, N1, STEP), lambda v, s: (v, 0, s)),
        ],
        out_specs=pl.BlockSpec((1, RANK, STEP), lambda v, s: (v, 0, s)),
        out_shape=jax.ShapeDtypeStruct((variables, RANK, columns), jnp.float32),
        compiler_params=pltpu.CompilerParams(vmem_limit_bytes=24 << 20),
    )(basis, field)


def spread(block, axes, size):
    return lax.all_to_all(jnp.broadcast_to(block, (size,) + block.shape), axes, 0, 0)


def all_sum(packed):
    core = lax.axis_index("core")
    half = packed.shape[0] // 2
    swap = [(0, 1), (1, 0)]
    mine = lax.dynamic_slice_in_dim(packed, core * half, half)
    theirs = lax.dynamic_slice_in_dim(packed, (1 - core) * half, half)
    own = mine + lax.ppermute(theirs, "core", swap)
    plane = lax.axis_size("y") * lax.axis_size("x")
    piece = half // plane
    pieces = lax.all_to_all(own.reshape(plane, piece, BLOCK), ("y", "x"), 0, 0)
    own = jnp.sum(pieces, axis=0)
    own = jnp.sum(spread(own, "z", lax.axis_size("z")), axis=0)
    own = spread(own, ("y", "x"), plane).reshape(half, BLOCK)
    return core, own, lax.ppermute(own, "core", swap)


def local(tensor_field, start_basis):
    packed = partial_gram(tensor_field).reshape(len(PAIRS) * BLOCK, BLOCK)
    core, own, other = all_sum(packed)
    basis = sweeps(core.astype(jnp.int32).reshape(1), own, other, start_basis)
    return project(basis, tensor_field), basis


def solution(mesh):
    fine = Mesh(mesh.devices.reshape(8, 4, 4, 2), ("z", "y", "x", "core"))
    spec = P(("x", "core"), None, ("z", "y"))
    return jax.shard_map(local, mesh=fine, in_specs=(spec, P()), out_specs=(spec, P()), check_vma=False)
```

```python
import jax
import jax.numpy as jnp
from jax import lax
from jax.experimental import pallas as pl
from jax.experimental.pallas import tpu as pltpu
from jax.sharding import Mesh, PartitionSpec as P

ITERS = 4
N1 = 512
RANK = 128
PANEL = 16
BLOCK = 128
PAIRS = [(i, j) for i in range(N1 // BLOCK) for j in range(i, N1 // BLOCK)]
HIGHEST = lax.Precision.HIGHEST
STEP = 512
TILE = (8, 128)


def split(values):
    high = values.astype(jnp.bfloat16)
    low = (values - high.astype(jnp.float32)).astype(jnp.bfloat16)
    return high, low


def dot(left, right, contract):
    return lax.dot_general(left, right, (contract, ((), ())), preferred_element_type=jnp.float32)


def gram_kernel(field_ref, out_ref, parts_ref, total_ref, arrived):
    nt = ((1,), (1,))
    variables, _, columns = field_ref.shape
    per = columns // STEP
    copies = [
        pltpu.make_async_copy(
            field_ref.at[c // per, :, pl.ds((c % per) * STEP, STEP)], parts_ref.at[c], arrived.at[c]
        )
        for c in range(variables * per)
    ]
    for copy in copies:
        copy.start()
    for c, copy in enumerate(copies):
        copy.wait()
        high, low = split(parts_ref[c])
        halved = high * jnp.bfloat16(0.5)
        term = dot(high, halved, nt) + dot(high, low, nt)
        if c == 0:
            total_ref[...] = term
        else:
            total_ref[...] += term
    scale = 1.0 / 524288
    for index, (i, j) in enumerate(PAIRS):
        rows = pl.ds(BLOCK * i, BLOCK)
        others = pl.ds(BLOCK * j, BLOCK)
        out_ref[index] = (total_ref[rows, others] + total_ref[others, rows].T) * scale


def partial_gram(field):
    variables, _, columns = field.shape
    parts = variables * columns // STEP
    return pl.pallas_call(
        gram_kernel,
        in_specs=[pl.BlockSpec(memory_space=pltpu.HBM)],
        out_specs=pl.BlockSpec(memory_space=pltpu.VMEM),
        out_shape=jax.ShapeDtypeStruct((len(PAIRS), BLOCK, BLOCK), jnp.float32),
        scratch_shapes=[
            pltpu.VMEM((parts, N1, STEP), jnp.float32),
            pltpu.VMEM((N1, N1), jnp.float32),
            pltpu.SemaphoreType.DMA((parts,)),
        ],
        compiler_params=pltpu.CompilerParams(vmem_limit_bytes=51 << 20),
    )(field)


def row_of(tile, k):
    return jnp.broadcast_to(tile[k : k + 1, :], TILE)


def lane_of(tile, k):
    return jnp.broadcast_to(tile[:, k : k + 1], TILE)


def inverse_factor(products, beside):
    tiles = PANEL // 8
    panels = RANK // PANEL
    row = lax.broadcasted_iota(jnp.int32, TILE, 0)
    lane = lax.broadcasted_iota(jnp.int32, TILE, 1)
    rows = [
        [products[PANEL * p + 8 * h : PANEL * p + 8 * h + 8, :] for h in range(tiles)] for p in range(panels)
    ]
    done = []
    for r in range(panels):
        first = PANEL * r
        last = r == panels - 1
        panel = rows[r] + ([] if last else rows[r + 1])
        height = len(panel)
        columns = [
            [lane_of(panel[h], first + k) if h >= k // 8 else None for h in range(height)]
            for k in range(PANEL)
        ]
        inside = (lane >= first) & (lane < first + PANEL)
        for h in range(height):
            unit = jnp.where(lane - (first + 8 * h) == row, 1.0, 0.0) if h < tiles else 0.0
            panel[h] = jnp.where(inside, unit, panel[h])
        scale = [None] * tiles
        pivot = row_of(columns[0][0], 0)
        for k in range(PANEL):
            g, at = divmod(k, 8)
            root = lax.rsqrt(pivot)
            scale[g] = root if at == 0 else jnp.where(row >= at, root, scale[g])
            if k == PANEL - 1 and last:
                break
            inverse = 1.0 / pivot
            if k < PANEL - 1:
                h, after = divmod(k + 1, 8)
                link = row_of(columns[k][h], after)
                pivot = row_of(columns[k + 1][h], after) - (link * link) * inverse
            below = [h for h in range(g, height) if not (h == g and at == 7)]
            factor = {
                h: (jnp.where(row > at, columns[k][h], 0.0) if h == g else columns[k][h]) * inverse
                for h in below
            }
            for j in range(k + 1, PANEL):
                across = row_of(columns[k][j // 8], j % 8)
                for h in below:
                    if h >= j // 8:
                        columns[j][h] = columns[j][h] - factor[h] * across
            across = row_of(panel[g], at)
            for h in below:
                panel[h] = panel[h] - factor[h] * across
        if not last:
            rows[r + 1] = panel[tiles:]
        panel = [panel[h] * scale[h] for h in range(tiles)]
        for h in range(tiles):
            done.append(jnp.where(lane < first + PANEL, panel[h], 0.0))
        beside(r)
        ahead = r + 2
        if ahead < panels:
            for h in range(tiles):
                update = None
                for i in range(8):
                    at = PANEL * ahead + 8 * h + i
                    term = sum(lane_of(panel[t], at) * panel[t] for t in range(tiles))
                    total = jnp.broadcast_to(jnp.sum(term, axis=0, keepdims=True), TILE)
                    update = total if i == 0 else jnp.where(row >= i, total, update)
                rows[ahead][h] = jnp.where(inside, 0.0, rows[ahead][h]) - update
        ahead = r + 3
        if ahead < panels:
            whole = jnp.concatenate(panel, axis=0)
            trail = exact_dot(whole[:, PANEL * ahead :], whole, ((0,), (0,)))
            for p in range(ahead, panels):
                for h in range(tiles):
                    at = PANEL * (p - ahead) + 8 * h
                    rows[p][h] = jnp.where(inside, 0.0, rows[p][h]) - trail[at : at + 8, :]
    return jnp.concatenate(done, axis=0)


def exact_dot(left, right, contract):
    return lax.dot_general(
        left, right, (contract, ((), ())), precision=HIGHEST, preferred_element_type=jnp.float32
    )


def split_three(values):
    high = values.astype(jnp.bfloat16)
    rest = values - high.astype(jnp.float32)
    middle = rest.astype(jnp.bfloat16)
    low = (rest - middle.astype(jnp.float32)).astype(jnp.bfloat16)
    return high, middle, low


def sweeps_kernel(
    core_ref,
    own_ref,
    other_ref,
    start_ref,
    field_ref,
    core_out_ref,
    basis_ref,
    gram_ref,
    wide_ref,
    image_ref,
    ahead_ref,
    parts_ref,
    results_ref,
    arrived,
    sent,
):
    nn, tn, nt = ((1,), (0,)), ((0,), (0,)), ((1,), (1,))
    variables, _, columns = field_ref.shape
    per = columns // STEP
    pieces = [(c // per, pl.ds((c % per) * STEP, STEP)) for c in range(variables * per)]
    fetches = [
        pltpu.make_async_copy(field_ref.at[v, :, span], parts_ref.at[c], arrived.at[c])
        for c, (v, span) in enumerate(pieces)
    ]
    for fetch in fetches:
        fetch.start()

    own_first = core_ref[0] == 0
    rows_half = own_ref.shape[0]
    for index, (i, j) in enumerate(PAIRS):
        at = (index * BLOCK) % rows_half
        own = own_ref[at : at + BLOCK, :]
        other = other_ref[at : at + BLOCK, :]
        block = jnp.where(own_first == (index * BLOCK < rows_half), own, other)
        for part, values in enumerate(split_three(block)):
            gram_ref[part, BLOCK * i : BLOCK * (i + 1), BLOCK * j : BLOCK * (j + 1)] = values
        if i != j:
            for part, values in enumerate(split_three(block.T)):
                gram_ref[part, BLOCK * j : BLOCK * (j + 1), BLOCK * i : BLOCK * (i + 1)] = values

    def widen(values):
        high, middle, low = split_three(values)
        wide_ref[:N1, :RANK] = high
        wide_ref[:N1, RANK:] = middle
        wide_ref[N1:, :RANK] = low

    def gram_times(at, size):
        span = pl.ds(at, size)
        wide = wide_ref[:N1, :]
        by_high = dot(gram_ref[0, span, :], wide, nn)
        by_middle = dot(gram_ref[1, span, :], wide, nn)
        small = dot(gram_ref[0, span, :], wide_ref[N1:, :RANK], nn) + dot(
            gram_ref[2, span, :], wide_ref[:N1, :RANK], nn
        )
        return by_high[:, :RANK] + (by_high[:, RANK:] + by_middle[:, :RANK] + (by_middle[:, RANK:] + small))

    widen(start_ref[...])
    image_ref[...] = gram_times(0, N1)

    def sweep(iteration, carry):
        image = image_ref[...]
        products = exact_dot(image, image, tn)
        widen(image)

        def beside(r):
            if r % 2 == 0:
                ahead_ref[64 * r : 64 * r + 128, :] = gram_times(64 * r, 128)

        inverse = inverse_factor(products, beside)
        image_ref[...] = exact_dot(ahead_ref[...], inverse, nt)
        return carry

    lax.fori_loop(0, ITERS - 1, sweep, 0)
    image = image_ref[...]
    products = exact_dot(image, image, tn)
    inverse = inverse_factor(products, lambda r: None)
    basis = exact_dot(image, inverse, nt)
    basis_ref[...] = basis
    basis_high, basis_low = split(basis)
    sends = [
        pltpu.make_async_copy(results_ref.at[c], core_out_ref.at[v, :, span], sent.at[c])
        for c, (v, span) in enumerate(pieces)
    ]
    for c in range(len(pieces)):
        fetches[c].wait()
        high, low = split(parts_ref[c])
        results_ref[c] = dot(basis_high, high, tn) + (dot(basis_high, low, tn) + dot(basis_low, high, tn))
        sends[c].start()
    for send in sends:
        send.wait()


def sweeps(core, own, other, start_basis, field):
    variables, _, columns = field.shape
    parts = variables * columns // STEP
    whole = pl.BlockSpec(memory_space=pltpu.VMEM)
    anywhere = pl.BlockSpec(memory_space=pltpu.HBM)
    return pl.pallas_call(
        sweeps_kernel,
        in_specs=[pl.BlockSpec(memory_space=pltpu.SMEM), whole, whole, whole, anywhere],
        out_specs=[anywhere, whole],
        out_shape=[
            jax.ShapeDtypeStruct((variables, RANK, columns), jnp.float32),
            jax.ShapeDtypeStruct((N1, RANK), jnp.float32),
        ],
        scratch_shapes=[
            pltpu.VMEM((3, N1, N1), jnp.bfloat16),
            pltpu.VMEM((2 * N1, 2 * RANK), jnp.bfloat16),
            pltpu.VMEM((N1, RANK), jnp.float32),
            pltpu.VMEM((N1, RANK), jnp.float32),
            pltpu.VMEM((parts, N1, STEP), jnp.float32),
            pltpu.VMEM((parts, RANK, STEP), jnp.float32),
            pltpu.SemaphoreType.DMA((parts,)),
            pltpu.SemaphoreType.DMA((parts,)),
        ],
        compiler_params=pltpu.CompilerParams(vmem_limit_bytes=51 << 20),
    )(core, own, other, start_basis, field)


def spread(block, axes, size):
    return lax.all_to_all(jnp.broadcast_to(block, (size,) + block.shape), axes, 0, 0)


def all_sum(packed):
    core = lax.axis_index("core")
    half = packed.shape[0] // 2
    swap = [(0, 1), (1, 0)]
    mine = lax.dynamic_slice_in_dim(packed, core * half, half)
    theirs = lax.dynamic_slice_in_dim(packed, (1 - core) * half, half)
    own = mine + lax.ppermute(theirs, "core", swap)
    plane = lax.axis_size("y") * lax.axis_size("x")
    piece = half // plane
    pieces = lax.all_to_all(own.reshape(plane, piece, BLOCK), ("y", "x"), 0, 0)
    own = jnp.sum(pieces, axis=0)
    own = jnp.sum(spread(own, "z", lax.axis_size("z")), axis=0)
    own = spread(own, ("y", "x"), plane).reshape(half, BLOCK)
    return core, own, lax.ppermute(own, "core", swap)


def local(tensor_field, start_basis):
    packed = partial_gram(tensor_field).reshape(len(PAIRS) * BLOCK, BLOCK)
    core, own, other = all_sum(packed)
    return tuple(sweeps(core.astype(jnp.int32).reshape(1), own, other, start_basis, tensor_field))


def solution(mesh):
    fine = Mesh(mesh.devices.reshape(8, 4, 4, 2), ("z", "y", "x", "core"))
    spec = P(("x", "core"), None, ("z", "y"))
    return jax.shard_map(local, mesh=fine, in_specs=(spec, P()), out_specs=(spec, P()), check_vma=False)
```

```python
import jax
import jax.numpy as jnp
from jax import lax
from jax.experimental import pallas as pl
from jax.experimental.pallas import tpu as pltpu
from jax.sharding import Mesh, PartitionSpec as P

ITERS = 4
N1 = 512
RANK = 128
PANEL = 16
BLOCK = 128
PAIRS = [(i, j) for i in range(N1 // BLOCK) for j in range(i, N1 // BLOCK)]
HIGHEST = lax.Precision.HIGHEST
STEP = 512
TILE = (8, 128)


def split(values):
    high = values.astype(jnp.bfloat16)
    low = (values - high.astype(jnp.float32)).astype(jnp.bfloat16)
    return high, low


def dot(left, right, contract):
    return lax.dot_general(left, right, (contract, ((), ())), preferred_element_type=jnp.float32)


def gram_kernel(field_ref, out_ref, parts_ref, total_ref, arrived):
    nt = ((1,), (1,))
    variables, _, columns = field_ref.shape
    per = columns // STEP
    copies = [
        pltpu.make_async_copy(
            field_ref.at[c // per, :, pl.ds((c % per) * STEP, STEP)], parts_ref.at[c], arrived.at[c]
        )
        for c in range(variables * per)
    ]
    for copy in copies:
        copy.start()
    for c, copy in enumerate(copies):
        copy.wait()
        high, low = split(parts_ref[c])
        halved = high * jnp.bfloat16(0.5)
        term = dot(high, halved, nt) + dot(high, low, nt)
        if c == 0:
            total_ref[...] = term
        else:
            total_ref[...] += term
    scale = 1.0 / 524288
    for index, (i, j) in enumerate(PAIRS):
        rows = pl.ds(BLOCK * i, BLOCK)
        others = pl.ds(BLOCK * j, BLOCK)
        out_ref[index] = (total_ref[rows, others] + total_ref[others, rows].T) * scale


def partial_gram(field):
    variables, _, columns = field.shape
    parts = variables * columns // STEP
    return pl.pallas_call(
        gram_kernel,
        in_specs=[pl.BlockSpec(memory_space=pltpu.HBM)],
        out_specs=pl.BlockSpec(memory_space=pltpu.VMEM),
        out_shape=jax.ShapeDtypeStruct((len(PAIRS), BLOCK, BLOCK), jnp.float32),
        scratch_shapes=[
            pltpu.VMEM((parts, N1, STEP), jnp.float32),
            pltpu.VMEM((N1, N1), jnp.float32),
            pltpu.SemaphoreType.DMA((parts,)),
        ],
        compiler_params=pltpu.CompilerParams(vmem_limit_bytes=51 << 20),
    )(field)


def row_of(tile, k):
    return jnp.broadcast_to(tile[k : k + 1, :], TILE)


def lane_of(tile, k):
    return jnp.broadcast_to(tile[:, k : k + 1], TILE)


def inverse_factor(products, beside):
    tiles = PANEL // 8
    panels = RANK // PANEL
    row = lax.broadcasted_iota(jnp.int32, TILE, 0)
    lane = lax.broadcasted_iota(jnp.int32, TILE, 1)
    rows = [
        [products[PANEL * p + 8 * h : PANEL * p + 8 * h + 8, :] for h in range(tiles)] for p in range(panels)
    ]
    done = []
    for r in range(panels):
        first = PANEL * r
        last = r == panels - 1
        panel = rows[r] + ([] if last else rows[r + 1])
        height = len(panel)
        columns = [
            [lane_of(panel[h], first + k) if h >= k // 8 else None for h in range(height)]
            for k in range(PANEL)
        ]
        inside = (lane >= first) & (lane < first + PANEL)
        for h in range(height):
            unit = jnp.where(lane - (first + 8 * h) == row, 1.0, 0.0) if h < tiles else 0.0
            panel[h] = jnp.where(inside, unit, panel[h])
        scale = [None] * tiles
        pivot = row_of(columns[0][0], 0)
        for k in range(PANEL):
            g, at = divmod(k, 8)
            root = lax.rsqrt(pivot)
            scale[g] = root if at == 0 else jnp.where(row >= at, root, scale[g])
            if k == PANEL - 1 and last:
                break
            inverse = 1.0 / pivot
            if k < PANEL - 1:
                h, after = divmod(k + 1, 8)
                link = row_of(columns[k][h], after)
                pivot = row_of(columns[k + 1][h], after) - (link * link) * inverse
            below = [h for h in range(g, height) if not (h == g and at == 7)]
            factor = {
                h: (jnp.where(row > at, columns[k][h], 0.0) if h == g else columns[k][h]) * inverse
                for h in below
            }
            for j in range(k + 1, PANEL):
                across = row_of(columns[k][j // 8], j % 8)
                for h in below:
                    if h >= j // 8:
                        columns[j][h] = columns[j][h] - factor[h] * across
            across = row_of(panel[g], at)
            for h in below:
                panel[h] = panel[h] - factor[h] * across
        if not last:
            rows[r + 1] = panel[tiles:]
        panel = [panel[h] * scale[h] for h in range(tiles)]
        for h in range(tiles):
            done.append(jnp.where(lane < first + PANEL, panel[h], 0.0))
        beside(r)
        ahead = r + 2
        if ahead < panels:
            for h in range(tiles):
                update = None
                for i in range(8):
                    at = PANEL * ahead + 8 * h + i
                    term = sum(lane_of(panel[t], at) * panel[t] for t in range(tiles))
                    total = jnp.broadcast_to(jnp.sum(term, axis=0, keepdims=True), TILE)
                    update = total if i == 0 else jnp.where(row >= i, total, update)
                rows[ahead][h] = jnp.where(inside, 0.0, rows[ahead][h]) - update
        ahead = r + 3
        if ahead < panels:
            whole = jnp.concatenate(panel, axis=0)
            trail = exact_dot(whole[:, PANEL * ahead :], whole, ((0,), (0,)))
            for p in range(ahead, panels):
                for h in range(tiles):
                    at = PANEL * (p - ahead) + 8 * h
                    rows[p][h] = jnp.where(inside, 0.0, rows[p][h]) - trail[at : at + 8, :]
    return jnp.concatenate(done, axis=0)


def exact_dot(left, right, contract):
    return lax.dot_general(
        left, right, (contract, ((), ())), precision=HIGHEST, preferred_element_type=jnp.float32
    )


def split_three(values):
    high = values.astype(jnp.bfloat16)
    rest = values - high.astype(jnp.float32)
    middle = rest.astype(jnp.bfloat16)
    low = (rest - middle.astype(jnp.float32)).astype(jnp.bfloat16)
    return high, middle, low


def sweeps_kernel(
    core_ref,
    own_ref,
    other_ref,
    start_ref,
    field_ref,
    core_out_ref,
    basis_ref,
    gram_ref,
    image_ref,
    ahead_ref,
    parts_ref,
    high_ref,
    low_ref,
    results_ref,
    arrived,
    sent,
):
    nn, nt = ((1,), (0,)), ((1,), (1,))
    variables, _, columns = field_ref.shape
    per = columns // STEP
    pieces = [(c // per, pl.ds((c % per) * STEP, STEP)) for c in range(variables * per)]
    fetches = [
        pltpu.make_async_copy(field_ref.at[v, :, span], parts_ref.at[c], arrived.at[c])
        for c, (v, span) in enumerate(pieces)
    ]
    for fetch in fetches:
        fetch.start()

    own_first = core_ref[0] == 0
    rows_half = own_ref.shape[0]
    for index, (i, j) in enumerate(PAIRS):
        at = (index * BLOCK) % rows_half
        own = own_ref[at : at + BLOCK, :]
        other = other_ref[at : at + BLOCK, :]
        block = jnp.where(own_first == (index * BLOCK < rows_half), own, other)
        for part, values in enumerate(split_three(block)):
            gram_ref[part, BLOCK * i : BLOCK * (i + 1), BLOCK * j : BLOCK * (j + 1)] = values
        if i != j:
            for part, values in enumerate(split_three(block.T)):
                gram_ref[part, BLOCK * j : BLOCK * (j + 1), BLOCK * i : BLOCK * (i + 1)] = values

    def keep(ref, values, at=0):
        for part, piece in enumerate(split_three(values)):
            ref[RANK * part : RANK * (part + 1), at : at + values.shape[1]] = piece

    def times_gram(at, size):
        span = pl.ds(at, size)
        by_high = dot(image_ref[...], gram_ref[0, :, span], nn)
        by_middle = dot(image_ref[: 2 * RANK, :], gram_ref[1, :, span], nn)
        by_low = dot(image_ref[:RANK, :], gram_ref[2, :, span], nn)
        small = by_middle[RANK:] + (by_high[2 * RANK :] + by_low)
        return by_high[:RANK] + (by_high[RANK : 2 * RANK] + by_middle[:RANK] + small)

    def products():
        both = dot(image_ref[...], image_ref[: 2 * RANK, :], nt)
        small = both[2 * RANK :, :RANK] + dot(image_ref[:RANK, :], image_ref[2 * RANK :, :], nt)
        middle = both[:RANK, RANK:] + both[RANK : 2 * RANK, :RANK]
        return both[:RANK, :RANK] + (middle + (both[RANK : 2 * RANK, RANK:] + small))

    def times_inverse(inverse, ref):
        high, middle, low = split_three(inverse)
        left = jnp.concatenate([high, low, middle, middle, high, high], axis=1)
        by_high, by_middle, by_low = (ref[RANK * part : RANK * (part + 1), :] for part in range(3))
        right = jnp.concatenate([by_low, by_high, by_middle, by_high, by_middle, by_high], axis=0)
        return dot(left, right, nn)

    keep(image_ref, start_ref[...].T)
    keep(image_ref, times_gram(0, N1))

    def sweep(iteration, carry):
        def beside(r):
            if r in (0, 2):
                keep(ahead_ref, times_gram(128 * r, 256), 128 * r)

        inverse = inverse_factor(products(), beside)
        keep(image_ref, times_inverse(inverse, ahead_ref))
        return carry

    lax.fori_loop(0, ITERS - 1, sweep, 0)

    def beside(r):
        if r < len(pieces):
            fetches[r].wait()
            high_ref[r], low_ref[r] = split(parts_ref[r])

    inverse = inverse_factor(products(), beside)
    basis = times_inverse(inverse, image_ref)
    basis_ref[...] = basis.T
    basis_high, basis_low = split(basis)
    basis_parts = jnp.concatenate([basis_high, basis_low], axis=0)
    sends = [
        pltpu.make_async_copy(results_ref.at[c], core_out_ref.at[v, :, span], sent.at[c])
        for c, (v, span) in enumerate(pieces)
    ]
    for c in range(len(pieces)):
        by_high = dot(basis_parts, high_ref[c], nn)
        results_ref[c] = by_high[:RANK] + (by_high[RANK:] + dot(basis_high, low_ref[c], nn))
        sends[c].start()
    for send in sends:
        send.wait()


def sweeps(core, own, other, start_basis, field):
    variables, _, columns = field.shape
    parts = variables * columns // STEP
    whole = pl.BlockSpec(memory_space=pltpu.VMEM)
    anywhere = pl.BlockSpec(memory_space=pltpu.HBM)
    return pl.pallas_call(
        sweeps_kernel,
        in_specs=[pl.BlockSpec(memory_space=pltpu.SMEM), whole, whole, whole, anywhere],
        out_specs=[anywhere, whole],
        out_shape=[
            jax.ShapeDtypeStruct((variables, RANK, columns), jnp.float32),
            jax.ShapeDtypeStruct((N1, RANK), jnp.float32),
        ],
        scratch_shapes=[
            pltpu.VMEM((3, N1, N1), jnp.bfloat16),
            pltpu.VMEM((3 * RANK, N1), jnp.bfloat16),
            pltpu.VMEM((3 * RANK, N1), jnp.bfloat16),
            pltpu.VMEM((parts, N1, STEP), jnp.float32),
            pltpu.VMEM((parts, N1, STEP), jnp.bfloat16),
            pltpu.VMEM((parts, N1, STEP), jnp.bfloat16),
            pltpu.VMEM((parts, RANK, STEP), jnp.float32),
            pltpu.SemaphoreType.DMA((parts,)),
            pltpu.SemaphoreType.DMA((parts,)),
        ],
        compiler_params=pltpu.CompilerParams(vmem_limit_bytes=51 << 20),
    )(core, own, other, start_basis, field)


def spread(block, axes, size):
    return lax.all_to_all(jnp.broadcast_to(block, (size,) + block.shape), axes, 0, 0)


def all_sum(packed):
    core = lax.axis_index("core")
    half = packed.shape[0] // 2
    swap = [(0, 1), (1, 0)]
    mine = lax.dynamic_slice_in_dim(packed, core * half, half)
    theirs = lax.dynamic_slice_in_dim(packed, (1 - core) * half, half)
    own = mine + lax.ppermute(theirs, "core", swap)
    plane = lax.axis_size("y") * lax.axis_size("x")
    piece = half // plane
    pieces = lax.all_to_all(own.reshape(plane, piece, BLOCK), ("y", "x"), 0, 0)
    own = jnp.sum(pieces, axis=0)
    own = jnp.sum(spread(own, "z", lax.axis_size("z")), axis=0)
    own = spread(own, ("y", "x"), plane).reshape(half, BLOCK)
    return core, own, lax.ppermute(own, "core", swap)


def local(tensor_field, start_basis):
    packed = partial_gram(tensor_field).reshape(len(PAIRS) * BLOCK, BLOCK)
    core, own, other = all_sum(packed)
    return tuple(sweeps(core.astype(jnp.int32).reshape(1), own, other, start_basis, tensor_field))


def solution(mesh):
    fine = Mesh(mesh.devices.reshape(8, 4, 4, 2), ("z", "y", "x", "core"))
    spec = P(("x", "core"), None, ("z", "y"))
    return jax.shard_map(local, mesh=fine, in_specs=(spec, P()), out_specs=(spec, P()), check_vma=False)
```

```python
import jax
import jax.numpy as jnp
from jax import lax
from jax.experimental import pallas as pl
from jax.experimental.pallas import tpu as pltpu
from jax.sharding import Mesh, PartitionSpec as P

ITERS = 4
N1 = 512
RANK = 128
PANEL = 16
BLOCK = 128
PAIRS = [(i, j) for i in range(N1 // BLOCK) for j in range(i, N1 // BLOCK)]
STEP = 512
TILE = (8, 128)


def split(values):
    high = values.astype(jnp.bfloat16)
    low = (values - high.astype(jnp.float32)).astype(jnp.bfloat16)
    return high, low


def dot(left, right, contract):
    return lax.dot_general(left, right, (contract, ((), ())), preferred_element_type=jnp.float32)


def gram_kernel(field_ref, out_ref, parts_ref, total_ref, arrived):
    nt = ((1,), (1,))
    variables, _, columns = field_ref.shape
    per = columns // STEP
    copies = [
        pltpu.make_async_copy(
            field_ref.at[c // per, :, pl.ds((c % per) * STEP, STEP)], parts_ref.at[c], arrived.at[c]
        )
        for c in range(variables * per)
    ]
    for copy in copies:
        copy.start()
    for c, copy in enumerate(copies):
        copy.wait()
        high, low = split(parts_ref[c])
        halved = high * jnp.bfloat16(0.5)
        term = dot(high, halved, nt) + dot(high, low, nt)
        if c == 0:
            total_ref[...] = term
        else:
            total_ref[...] += term
    scale = 1.0 / 524288
    for index, (i, j) in enumerate(PAIRS):
        rows = pl.ds(BLOCK * i, BLOCK)
        others = pl.ds(BLOCK * j, BLOCK)
        out_ref[index] = (total_ref[rows, others] + total_ref[others, rows].T) * scale


def partial_gram(field):
    variables, _, columns = field.shape
    parts = variables * columns // STEP
    return pl.pallas_call(
        gram_kernel,
        in_specs=[pl.BlockSpec(memory_space=pltpu.HBM)],
        out_specs=pl.BlockSpec(memory_space=pltpu.VMEM),
        out_shape=jax.ShapeDtypeStruct((len(PAIRS), BLOCK, BLOCK), jnp.float32),
        scratch_shapes=[
            pltpu.VMEM((parts, N1, STEP), jnp.float32),
            pltpu.VMEM((N1, N1), jnp.float32),
            pltpu.SemaphoreType.DMA((parts,)),
        ],
        compiler_params=pltpu.CompilerParams(vmem_limit_bytes=51 << 20),
    )(field)


def row_of(tile, k):
    return jnp.broadcast_to(tile[k : k + 1, :], TILE)


def lane_of(tile, k):
    return jnp.broadcast_to(tile[:, k : k + 1], TILE)


def inverse_factor(products, beside):
    tiles = PANEL // 8
    panels = RANK // PANEL
    row = lax.broadcasted_iota(jnp.int32, TILE, 0)
    lane = lax.broadcasted_iota(jnp.int32, TILE, 1)
    rows = [
        [products[PANEL * p + 8 * h : PANEL * p + 8 * h + 8, :] for h in range(tiles)] for p in range(panels)
    ]
    done = []
    for r in range(panels):
        first = PANEL * r
        last = r == panels - 1
        panel = rows[r] + ([] if last else rows[r + 1])
        height = len(panel)
        columns = [
            [lane_of(panel[h], first + k) if h >= k // 8 else None for h in range(height)]
            for k in range(PANEL)
        ]
        inside = (lane >= first) & (lane < first + PANEL)
        for h in range(height):
            unit = jnp.where(lane - (first + 8 * h) == row, 1.0, 0.0) if h < tiles else 0.0
            panel[h] = jnp.where(inside, unit, panel[h])
        scale = [None] * tiles
        pivot = row_of(columns[0][0], 0)
        for k in range(PANEL):
            g, at = divmod(k, 8)
            root = lax.rsqrt(pivot)
            scale[g] = root if at == 0 else jnp.where(row >= at, root, scale[g])
            if k == PANEL - 1 and last:
                break
            inverse = 1.0 / pivot
            if k < PANEL - 1:
                h, after = divmod(k + 1, 8)
                link = row_of(columns[k][h], after)
                pivot = row_of(columns[k + 1][h], after) - (link * link) * inverse
            below = [h for h in range(g, height) if not (h == g and at == 7)]
            factor = {
                h: (jnp.where(row > at, columns[k][h], 0.0) if h == g else columns[k][h]) * inverse
                for h in below
            }
            for j in range(k + 1, PANEL):
                across = row_of(columns[k][j // 8], j % 8)
                for h in below:
                    if h >= j // 8:
                        columns[j][h] = columns[j][h] - factor[h] * across
            across = row_of(panel[g], at)
            for h in below:
                panel[h] = panel[h] - factor[h] * across
        if not last:
            rows[r + 1] = panel[tiles:]
        panel = [panel[h] * scale[h] for h in range(tiles)]
        for h in range(tiles):
            done.append(jnp.where(lane < first + PANEL, panel[h], 0.0))
        beside(r)
        ahead = r + 2
        if ahead < panels:
            high, middle, low = split_three(jnp.concatenate(panel, axis=0))
            left = jnp.concatenate([high, low, middle, middle, high, high], axis=0)
            right = jnp.concatenate([low, high, middle, high, middle, high], axis=0)
            trail = dot(left, right, ((0,), (0,)))
            for p in range(ahead, panels):
                for h in range(tiles):
                    at = PANEL * p + 8 * h
                    rows[p][h] = jnp.where(inside, 0.0, rows[p][h]) - trail[at : at + 8, :]
    return jnp.concatenate(done, axis=0)


def split_three(values):
    high = values.astype(jnp.bfloat16)
    rest = values - high.astype(jnp.float32)
    middle = rest.astype(jnp.bfloat16)
    low = (rest - middle.astype(jnp.float32)).astype(jnp.bfloat16)
    return high, middle, low


def sweeps_kernel(
    core_ref,
    own_ref,
    other_ref,
    start_ref,
    field_ref,
    core_out_ref,
    basis_ref,
    gram_ref,
    image_ref,
    ahead_ref,
    parts_ref,
    high_ref,
    low_ref,
    results_ref,
    result_ref,
    arrived,
    sent,
    basis_sent,
):
    nn, nt = ((1,), (0,)), ((1,), (1,))
    variables, _, columns = field_ref.shape
    per = columns // STEP
    pieces = [(c // per, pl.ds((c % per) * STEP, STEP)) for c in range(variables * per)]
    fetches = [
        pltpu.make_async_copy(field_ref.at[v, :, span], parts_ref.at[c], arrived.at[c])
        for c, (v, span) in enumerate(pieces)
    ]
    for fetch in fetches:
        fetch.start()

    own_first = core_ref[0] == 0
    rows_half = own_ref.shape[0]
    for index, (i, j) in enumerate(PAIRS):
        at = (index * BLOCK) % rows_half
        own = own_ref[at : at + BLOCK, :]
        other = other_ref[at : at + BLOCK, :]
        block = jnp.where(own_first == (index * BLOCK < rows_half), own, other)
        for part, values in enumerate(split_three(block)):
            gram_ref[part, BLOCK * i : BLOCK * (i + 1), BLOCK * j : BLOCK * (j + 1)] = values
        if i != j:
            for part, values in enumerate(split_three(block.T)):
                gram_ref[part, BLOCK * j : BLOCK * (j + 1), BLOCK * i : BLOCK * (i + 1)] = values

    def keep(ref, values, at=0):
        for part, piece in enumerate(split_three(values)):
            ref[RANK * part : RANK * (part + 1), at : at + values.shape[1]] = piece

    def times_gram(at, size):
        span = pl.ds(at, size)
        by_high = dot(image_ref[...], gram_ref[0, :, span], nn)
        by_middle = dot(image_ref[: 2 * RANK, :], gram_ref[1, :, span], nn)
        by_low = dot(image_ref[:RANK, :], gram_ref[2, :, span], nn)
        small = by_middle[RANK:] + (by_high[2 * RANK :] + by_low)
        return by_high[:RANK] + (by_high[RANK : 2 * RANK] + by_middle[:RANK] + small)

    def products():
        both = dot(image_ref[...], image_ref[: 2 * RANK, :], nt)
        small = both[2 * RANK :, :RANK] + dot(image_ref[:RANK, :], image_ref[2 * RANK :, :], nt)
        middle = both[:RANK, RANK:] + both[RANK : 2 * RANK, :RANK]
        return both[:RANK, :RANK] + (middle + (both[RANK : 2 * RANK, RANK:] + small))

    def times_inverse(inverse, ref):
        high, middle, low = split_three(inverse)
        left = jnp.concatenate([high, low, middle, middle, high, high], axis=1)
        by_high, by_middle, by_low = (ref[RANK * part : RANK * (part + 1), :] for part in range(3))
        right = jnp.concatenate([by_low, by_high, by_middle, by_high, by_middle, by_high], axis=0)
        return dot(left, right, nn)

    keep(image_ref, start_ref[...].T)
    keep(image_ref, times_gram(0, N1))

    def sweep(iteration, carry):
        def beside(r):
            if r in (0, 2):
                keep(ahead_ref, times_gram(128 * r, 256), 128 * r)

        inverse = inverse_factor(products(), beside)
        keep(image_ref, times_inverse(inverse, ahead_ref))
        return carry

    lax.fori_loop(0, ITERS - 1, sweep, 0)

    for fetch in fetches:
        fetch.wait()

    def beside(r):
        if r < len(pieces):
            high_ref[r], low_ref[r] = split(parts_ref[r])

    inverse = inverse_factor(products(), beside)
    basis = times_inverse(inverse, image_ref)
    result_ref[...] = basis.T
    basis_send = pltpu.make_async_copy(result_ref, basis_ref, basis_sent)
    basis_send.start()
    basis_high, basis_low = split(basis)
    basis_parts = jnp.concatenate([basis_high, basis_low], axis=0)
    sends = [
        pltpu.make_async_copy(results_ref.at[c], core_out_ref.at[v, :, span], sent.at[c])
        for c, (v, span) in enumerate(pieces)
    ]
    for c in range(len(pieces)):
        by_high = dot(basis_parts, high_ref[c], nn)
        results_ref[c] = by_high[:RANK] + (by_high[RANK:] + dot(basis_high, low_ref[c], nn))
        sends[c].start()
    basis_send.wait()
    for send in sends:
        send.wait()


def sweeps(core, own, other, start_basis, field):
    variables, _, columns = field.shape
    parts = variables * columns // STEP
    whole = pl.BlockSpec(memory_space=pltpu.VMEM)
    anywhere = pl.BlockSpec(memory_space=pltpu.HBM)
    return pl.pallas_call(
        sweeps_kernel,
        in_specs=[pl.BlockSpec(memory_space=pltpu.SMEM), whole, whole, whole, anywhere],
        out_specs=[anywhere, anywhere],
        out_shape=[
            jax.ShapeDtypeStruct((variables, RANK, columns), jnp.float32),
            jax.ShapeDtypeStruct((N1, RANK), jnp.float32),
        ],
        scratch_shapes=[
            pltpu.VMEM((3, N1, N1), jnp.bfloat16),
            pltpu.VMEM((3 * RANK, N1), jnp.bfloat16),
            pltpu.VMEM((3 * RANK, N1), jnp.bfloat16),
            pltpu.VMEM((parts, N1, STEP), jnp.float32),
            pltpu.VMEM((parts, N1, STEP), jnp.bfloat16),
            pltpu.VMEM((parts, N1, STEP), jnp.bfloat16),
            pltpu.VMEM((parts, RANK, STEP), jnp.float32),
            pltpu.VMEM((N1, RANK), jnp.float32),
            pltpu.SemaphoreType.DMA((parts,)),
            pltpu.SemaphoreType.DMA((parts,)),
            pltpu.SemaphoreType.DMA,
        ],
        compiler_params=pltpu.CompilerParams(vmem_limit_bytes=51 << 20),
    )(core, own, other, start_basis, field)


def spread(block, axes, size):
    return lax.all_to_all(jnp.broadcast_to(block, (size,) + block.shape), axes, 0, 0)


def all_sum(packed):
    core = lax.axis_index("core")
    half = packed.shape[0] // 2
    swap = [(0, 1), (1, 0)]
    mine = lax.dynamic_slice_in_dim(packed, core * half, half)
    theirs = lax.dynamic_slice_in_dim(packed, (1 - core) * half, half)
    own = mine + lax.ppermute(theirs, "core", swap)
    plane = lax.axis_size("y") * lax.axis_size("x")
    piece = half // plane
    pieces = lax.all_to_all(own.reshape(plane, piece, BLOCK), ("y", "x"), 0, 0)
    own = jnp.sum(pieces, axis=0)
    own = jnp.sum(spread(own, "z", lax.axis_size("z")), axis=0)
    own = spread(own, ("y", "x"), plane).reshape(half, BLOCK)
    return core, own, lax.ppermute(own, "core", swap)


def local(tensor_field, start_basis):
    packed = partial_gram(tensor_field).reshape(len(PAIRS) * BLOCK, BLOCK)
    core, own, other = all_sum(packed)
    return tuple(sweeps(core.astype(jnp.int32).reshape(1), own, other, start_basis, tensor_field))


def solution(mesh):
    fine = Mesh(mesh.devices.reshape(8, 4, 4, 2), ("z", "y", "x", "core"))
    spec = P(("x", "core"), None, ("z", "y"))
    return jax.shard_map(local, mesh=fine, in_specs=(spec, P()), out_specs=(spec, P()), check_vma=False)
```

```python
import jax
import jax.numpy as jnp
from jax import lax
from jax.experimental import pallas as pl
from jax.experimental.pallas import tpu as pltpu
from jax.sharding import Mesh, PartitionSpec as P

ITERS = 4
N1 = 512
RANK = 128
PANEL = 16
BLOCK = 128
PAIRS = [(i, j) for i in range(N1 // BLOCK) for j in range(i, N1 // BLOCK)]
STEP = 512
TILE = (8, 128)


def split(values):
    high = values.astype(jnp.bfloat16)
    low = (values - high.astype(jnp.float32)).astype(jnp.bfloat16)
    return high, low


def dot(left, right, contract):
    return lax.dot_general(left, right, (contract, ((), ())), preferred_element_type=jnp.float32)


def gram_kernel(field_ref, out_ref, parts_ref, total_ref, arrived):
    nt = ((1,), (1,))
    variables, _, columns = field_ref.shape
    per = columns // STEP
    copies = [
        pltpu.make_async_copy(
            field_ref.at[c // per, :, pl.ds((c % per) * STEP, STEP)], parts_ref.at[c], arrived.at[c]
        )
        for c in range(variables * per)
    ]
    for copy in copies:
        copy.start()
    for c, copy in enumerate(copies):
        copy.wait()
        high, low = split(parts_ref[c])
        halved = high * jnp.bfloat16(0.5)
        term = dot(high, halved, nt) + dot(high, low, nt)
        if c == 0:
            total_ref[...] = term
        else:
            total_ref[...] += term
    scale = 1.0 / 524288
    for index, (i, j) in enumerate(PAIRS):
        rows = pl.ds(BLOCK * i, BLOCK)
        others = pl.ds(BLOCK * j, BLOCK)
        out_ref[index] = (total_ref[rows, others] + total_ref[others, rows].T) * scale


def partial_gram(field):
    variables, _, columns = field.shape
    parts = variables * columns // STEP
    return pl.pallas_call(
        gram_kernel,
        in_specs=[pl.BlockSpec(memory_space=pltpu.HBM)],
        out_specs=pl.BlockSpec(memory_space=pltpu.VMEM),
        out_shape=jax.ShapeDtypeStruct((len(PAIRS), BLOCK, BLOCK), jnp.float32),
        scratch_shapes=[
            pltpu.VMEM((parts, N1, STEP), jnp.float32),
            pltpu.VMEM((N1, N1), jnp.float32),
            pltpu.SemaphoreType.DMA((parts,)),
        ],
        compiler_params=pltpu.CompilerParams(vmem_limit_bytes=51 << 20),
    )(field)


def row_of(tile, k):
    return jnp.broadcast_to(tile[k : k + 1, :], TILE)


def lane_of(tile, k):
    return jnp.broadcast_to(tile[:, k : k + 1], TILE)


def inverse_factor(products, beside):
    tiles = PANEL // 8
    panels = RANK // PANEL
    row = lax.broadcasted_iota(jnp.int32, TILE, 0)
    lane = lax.broadcasted_iota(jnp.int32, TILE, 1)
    rows = [
        [products[PANEL * p + 8 * h : PANEL * p + 8 * h + 8, :] for h in range(tiles)] for p in range(panels)
    ]
    done = []
    for r in range(panels):
        first = PANEL * r
        last = r == panels - 1
        panel = rows[r] + ([] if last else rows[r + 1])
        height = len(panel)
        columns = [
            [lane_of(panel[h], first + k) if h >= k // 8 else None for h in range(height)]
            for k in range(PANEL)
        ]
        inside = (lane >= first) & (lane < first + PANEL)
        for h in range(height):
            unit = jnp.where(lane - (first + 8 * h) == row, 1.0, 0.0) if h < tiles else 0.0
            panel[h] = jnp.where(inside, unit, panel[h])
        scale = [None] * tiles
        pivot = row_of(columns[0][0], 0)
        for k in range(PANEL):
            g, at = divmod(k, 8)
            root = lax.rsqrt(pivot)
            scale[g] = root if at == 0 else jnp.where(row >= at, root, scale[g])
            if k == PANEL - 1 and last:
                break
            inverse = 1.0 / pivot
            if k < PANEL - 1:
                h, after = divmod(k + 1, 8)
                link = row_of(columns[k][h], after)
                pivot = row_of(columns[k + 1][h], after) - (link * link) * inverse
            below = [h for h in range(g, height) if not (h == g and at == 7)]
            factor = {
                h: (jnp.where(row > at, columns[k][h], 0.0) if h == g else columns[k][h]) * inverse
                for h in below
            }
            for j in range(k + 1, PANEL):
                across = row_of(columns[k][j // 8], j % 8)
                for h in below:
                    if h >= j // 8:
                        columns[j][h] = columns[j][h] - factor[h] * across
            across = row_of(panel[g], at)
            for h in below:
                panel[h] = panel[h] - factor[h] * across
        if not last:
            rows[r + 1] = panel[tiles:]
        panel = [panel[h] * scale[h] for h in range(tiles)]
        for h in range(tiles):
            done.append(jnp.where(lane < first + PANEL, panel[h], 0.0))
        beside(r)
        ahead = r + 2
        if ahead < panels:
            high, middle, low = split_three(jnp.concatenate(panel, axis=0))
            left = jnp.concatenate([high, low, middle, middle, high, high], axis=0)
            right = jnp.concatenate([low, high, middle, high, middle, high], axis=0)
            trail = dot(left, right, ((0,), (0,)))
            for p in range(ahead, panels):
                for h in range(tiles):
                    at = PANEL * p + 8 * h
                    rows[p][h] = jnp.where(inside, 0.0, rows[p][h]) - trail[at : at + 8, :]
    return jnp.concatenate(done, axis=0)


def split_three(values):
    high = values.astype(jnp.bfloat16)
    rest = values - high.astype(jnp.float32)
    middle = rest.astype(jnp.bfloat16)
    low = (rest - middle.astype(jnp.float32)).astype(jnp.bfloat16)
    return high, middle, low


def sweeps_kernel(
    core_ref,
    own_ref,
    other_ref,
    start_ref,
    field_ref,
    core_out_ref,
    basis_ref,
    gram_ref,
    image_ref,
    ahead_ref,
    parts_ref,
    high_ref,
    low_ref,
    results_ref,
    result_ref,
    arrived,
    sent,
    basis_sent,
):
    nn, nt = ((1,), (0,)), ((1,), (1,))
    variables, _, columns = field_ref.shape
    per = columns // STEP
    pieces = [(c // per, pl.ds((c % per) * STEP, STEP)) for c in range(variables * per)]
    fetches = [
        pltpu.make_async_copy(field_ref.at[v, :, span], parts_ref.at[c], arrived.at[c])
        for c, (v, span) in enumerate(pieces)
    ]
    for fetch in fetches:
        fetch.start()

    own_first = core_ref[0] == 0
    rows_half = own_ref.shape[0]
    for index, (i, j) in enumerate(PAIRS):
        at = (index * BLOCK) % rows_half
        own = own_ref[at : at + BLOCK, :]
        other = other_ref[at : at + BLOCK, :]
        block = jnp.where(own_first == (index * BLOCK < rows_half), own, other)
        for part, values in enumerate(split_three(block)):
            gram_ref[part, BLOCK * i : BLOCK * (i + 1), BLOCK * j : BLOCK * (j + 1)] = values
        if i != j:
            for part, values in enumerate(split_three(block.T)):
                gram_ref[part, BLOCK * j : BLOCK * (j + 1), BLOCK * i : BLOCK * (i + 1)] = values

    def keep(ref, values, at=0):
        for part, piece in enumerate(split_three(values)):
            ref[RANK * part : RANK * (part + 1), at : at + values.shape[1]] = piece

    def times_gram(at, size):
        span = pl.ds(at, size)
        by_high = dot(image_ref[...], gram_ref[0, :, span], nn)
        by_middle = dot(image_ref[: 2 * RANK, :], gram_ref[1, :, span], nn)
        by_low = dot(image_ref[:RANK, :], gram_ref[2, :, span], nn)
        small = by_middle[RANK:] + (by_high[2 * RANK :] + by_low)
        return by_high[:RANK] + (by_high[RANK : 2 * RANK] + by_middle[:RANK] + small)

    def products():
        both = dot(image_ref[...], image_ref[: 2 * RANK, :], nt)
        small = both[2 * RANK :, :RANK] + dot(image_ref[:RANK, :], image_ref[2 * RANK :, :], nt)
        middle = both[:RANK, RANK:] + both[RANK : 2 * RANK, :RANK]
        return both[:RANK, :RANK] + (middle + (both[RANK : 2 * RANK, RANK:] + small))

    def times_inverse(inverse, ref):
        high, middle, low = split_three(inverse)
        left = jnp.concatenate([high, low, middle, middle, high, high], axis=1)
        by_high, by_middle, by_low = (ref[RANK * part : RANK * (part + 1), :] for part in range(3))
        right = jnp.concatenate([by_low, by_high, by_middle, by_high, by_middle, by_high], axis=0)
        return dot(left, right, nn)

    keep(image_ref, start_ref[...].T)
    keep(image_ref, times_gram(0, N1))

    def sweep(iteration, carry):
        def beside(r):
            if r in (0, 2):
                keep(ahead_ref, times_gram(128 * r, 256), 128 * r)

        inverse = inverse_factor(products(), beside)
        keep(image_ref, times_inverse(inverse, ahead_ref))
        return carry

    lax.fori_loop(0, ITERS - 1, sweep, 0)

    for fetch in fetches:
        fetch.wait()

    def beside(r):
        if r < len(pieces):
            high_ref[r], low_ref[r] = split(parts_ref[r])

    inverse = inverse_factor(products(), beside)
    basis = times_inverse(inverse, image_ref)
    result_ref[...] = basis.T
    basis_send = pltpu.make_async_copy(result_ref, basis_ref, basis_sent)
    basis_send.start()
    basis_high, basis_low = split(basis)
    basis_parts = jnp.concatenate([basis_high, basis_low], axis=0)
    sends = [
        pltpu.make_async_copy(results_ref.at[c], core_out_ref.at[v, :, span], sent.at[c])
        for c, (v, span) in enumerate(pieces)
    ]
    for c in range(len(pieces)):
        by_high = dot(basis_parts, high_ref[c], nn)
        results_ref[c] = by_high[:RANK] + (by_high[RANK:] + dot(basis_high, low_ref[c], nn))
        sends[c].start()
    basis_send.wait()
    for send in sends:
        send.wait()


def sweeps(core, own, other, start_basis, field):
    variables, _, columns = field.shape
    parts = variables * columns // STEP
    whole = pl.BlockSpec(memory_space=pltpu.VMEM)
    anywhere = pl.BlockSpec(memory_space=pltpu.HBM)
    return pl.pallas_call(
        sweeps_kernel,
        in_specs=[pl.BlockSpec(memory_space=pltpu.SMEM), whole, whole, whole, anywhere],
        out_specs=[anywhere, anywhere],
        out_shape=[
            jax.ShapeDtypeStruct((variables, RANK, columns), jnp.float32),
            jax.ShapeDtypeStruct((N1, RANK), jnp.float32),
        ],
        scratch_shapes=[
            pltpu.VMEM((3, N1, N1), jnp.bfloat16),
            pltpu.VMEM((3 * RANK, N1), jnp.bfloat16),
            pltpu.VMEM((3 * RANK, N1), jnp.bfloat16),
            pltpu.VMEM((parts, N1, STEP), jnp.float32),
            pltpu.VMEM((parts, N1, STEP), jnp.bfloat16),
            pltpu.VMEM((parts, N1, STEP), jnp.bfloat16),
            pltpu.VMEM((parts, RANK, STEP), jnp.float32),
            pltpu.VMEM((N1, RANK), jnp.float32),
            pltpu.SemaphoreType.DMA((parts,)),
            pltpu.SemaphoreType.DMA((parts,)),
            pltpu.SemaphoreType.DMA,
        ],
        compiler_params=pltpu.CompilerParams(vmem_limit_bytes=51 << 20),
    )(core, own, other, start_basis, field)


def spread(block, axes, size):
    return lax.all_to_all(jnp.broadcast_to(block, (size,) + block.shape), axes, 0, 0)


def all_sum(packed):
    core = lax.axis_index("core")
    half = packed.shape[0] // 2
    swap = [(0, 1), (1, 0)]
    mine = lax.dynamic_slice_in_dim(packed, core * half, half)
    theirs = lax.dynamic_slice_in_dim(packed, (1 - core) * half, half)
    own = mine + lax.ppermute(theirs, "core", swap)
    plane = lax.axis_size("y") * lax.axis_size("x")
    piece = half // plane
    pieces = lax.all_to_all(own.reshape(plane, piece, BLOCK), ("y", "x"), 0, 0)
    own = jnp.sum(pieces, axis=0)
    for flip in (1, 2, 7):
        own = own + lax.ppermute(own, "z", [(i, i ^ flip) for i in range(lax.axis_size("z"))])
    own = spread(own, ("y", "x"), plane).reshape(half, BLOCK)
    return core, own, lax.ppermute(own, "core", swap)


def local(tensor_field, start_basis):
    packed = partial_gram(tensor_field).reshape(len(PAIRS) * BLOCK, BLOCK)
    core, own, other = all_sum(packed)
    return tuple(sweeps(core.astype(jnp.int32).reshape(1), own, other, start_basis, tensor_field))


def solution(mesh):
    fine = Mesh(mesh.devices.reshape(8, 4, 4, 2), ("z", "y", "x", "core"))
    spec = P(("x", "core"), None, ("z", "y"))
    return jax.shard_map(local, mesh=fine, in_specs=(spec, P()), out_specs=(spec, P()), check_vma=False)
```

```python
import jax
import jax.numpy as jnp
from jax import lax
from jax.experimental import pallas as pl
from jax.experimental.pallas import tpu as pltpu
from jax.sharding import Mesh, PartitionSpec as P

ITERS = 4
N1 = 512
RANK = 128
PANEL = 16
BLOCK = 128
PAIRS = [(i, j) for i in range(N1 // BLOCK) for j in range(i, N1 // BLOCK)]
STEP = 512
TILE = (8, 128)


def split(values):
    high = values.astype(jnp.bfloat16)
    low = (values - high.astype(jnp.float32)).astype(jnp.bfloat16)
    return high, low


def dot(left, right, contract):
    return lax.dot_general(left, right, (contract, ((), ())), preferred_element_type=jnp.float32)


def gram_kernel(field_ref, out_ref, parts_ref, total_ref, arrived):
    nt = ((1,), (1,))
    variables, _, columns = field_ref.shape
    per = columns // STEP
    copies = [
        pltpu.make_async_copy(
            field_ref.at[c // per, :, pl.ds((c % per) * STEP, STEP)], parts_ref.at[c], arrived.at[c]
        )
        for c in range(variables * per)
    ]
    for copy in copies:
        copy.start()
    for c, copy in enumerate(copies):
        copy.wait()
        high, low = split(parts_ref[c])
        halved = high * jnp.bfloat16(0.5)
        term = dot(high, halved, nt) + dot(high, low, nt)
        if c == 0:
            total_ref[...] = term
        else:
            total_ref[...] += term
    scale = 1.0 / 524288
    for index, (i, j) in enumerate(PAIRS):
        rows = pl.ds(BLOCK * i, BLOCK)
        others = pl.ds(BLOCK * j, BLOCK)
        out_ref[index] = (total_ref[rows, others] + total_ref[others, rows].T) * scale


def partial_gram(field):
    variables, _, columns = field.shape
    parts = variables * columns // STEP
    return pl.pallas_call(
        gram_kernel,
        in_specs=[pl.BlockSpec(memory_space=pltpu.HBM)],
        out_specs=pl.BlockSpec(memory_space=pltpu.VMEM),
        out_shape=jax.ShapeDtypeStruct((len(PAIRS), BLOCK, BLOCK), jnp.float32),
        scratch_shapes=[
            pltpu.VMEM((parts, N1, STEP), jnp.float32),
            pltpu.VMEM((N1, N1), jnp.float32),
            pltpu.SemaphoreType.DMA((parts,)),
        ],
        compiler_params=pltpu.CompilerParams(vmem_limit_bytes=51 << 20),
    )(field)


def row_of(tile, k):
    return jnp.broadcast_to(tile[k : k + 1, :], TILE)


def lane_of(tile, k):
    return jnp.broadcast_to(tile[:, k : k + 1], TILE)


def inverse_factor(products, beside):
    tiles = PANEL // 8
    panels = RANK // PANEL
    row = lax.broadcasted_iota(jnp.int32, TILE, 0)
    lane = lax.broadcasted_iota(jnp.int32, TILE, 1)
    rows = [
        [products[PANEL * p + 8 * h : PANEL * p + 8 * h + 8, :] for h in range(tiles)] for p in range(panels)
    ]
    done = []
    for r in range(panels):
        first = PANEL * r
        last = r == panels - 1
        panel = rows[r] + ([] if last else rows[r + 1])
        height = len(panel)
        columns = [
            [lane_of(panel[h], first + k) if h >= k // 8 else None for h in range(height)]
            for k in range(PANEL)
        ]
        inside = (lane >= first) & (lane < first + PANEL)
        for h in range(height):
            unit = jnp.where(lane - (first + 8 * h) == row, 1.0, 0.0) if h < tiles else 0.0
            panel[h] = jnp.where(inside, unit, panel[h])
        scale = [None] * tiles
        pivot = row_of(columns[0][0], 0)
        for k in range(PANEL):
            g, at = divmod(k, 8)
            root = lax.rsqrt(pivot)
            scale[g] = root if at == 0 else jnp.where(row >= at, root, scale[g])
            if k == PANEL - 1 and last:
                break
            inverse = 1.0 / pivot
            if k < PANEL - 1:
                h, after = divmod(k + 1, 8)
                link = row_of(columns[k][h], after)
                pivot = row_of(columns[k + 1][h], after) - (link * link) * inverse
            below = [h for h in range(g, height) if not (h == g and at == 7)]
            factor = {
                h: (jnp.where(row > at, columns[k][h], 0.0) if h == g else columns[k][h]) * inverse
                for h in below
            }
            for j in range(k + 1, PANEL):
                across = row_of(columns[k][j // 8], j % 8)
                for h in below:
                    if h >= j // 8:
                        columns[j][h] = columns[j][h] - factor[h] * across
            across = row_of(panel[g], at)
            for h in below:
                panel[h] = panel[h] - factor[h] * across
        if not last:
            rows[r + 1] = panel[tiles:]
        panel = [panel[h] * scale[h] for h in range(tiles)]
        for h in range(tiles):
            done.append(jnp.where(lane < first + PANEL, panel[h], 0.0))
        beside(r)
        ahead = r + 2
        if ahead < panels:
            high, middle, low = split_three(jnp.concatenate(panel, axis=0))
            left = jnp.concatenate([high, low, middle, middle, high, high], axis=0)
            right = jnp.concatenate([low, high, middle, high, middle, high], axis=0)
            trail = dot(left, right, ((0,), (0,)))
            for p in range(ahead, panels):
                for h in range(tiles):
                    at = PANEL * p + 8 * h
                    rows[p][h] = jnp.where(inside, 0.0, rows[p][h]) - trail[at : at + 8, :]
    return jnp.concatenate(done, axis=0)


def split_three(values):
    high = values.astype(jnp.bfloat16)
    rest = values - high.astype(jnp.float32)
    middle = rest.astype(jnp.bfloat16)
    low = (rest - middle.astype(jnp.float32)).astype(jnp.bfloat16)
    return high, middle, low


def sweeps_kernel(
    core_ref,
    own_ref,
    other_ref,
    start_ref,
    field_ref,
    core_out_ref,
    basis_ref,
    gram_ref,
    image_ref,
    ahead_ref,
    parts_ref,
    high_ref,
    low_ref,
    results_ref,
    result_ref,
    arrived,
    sent,
    basis_sent,
):
    nn, nt = ((1,), (0,)), ((1,), (1,))
    variables, _, columns = field_ref.shape
    per = columns // STEP
    pieces = [(c // per, pl.ds((c % per) * STEP, STEP)) for c in range(variables * per)]
    fetches = [
        pltpu.make_async_copy(field_ref.at[v, :, span], parts_ref.at[c], arrived.at[c])
        for c, (v, span) in enumerate(pieces)
    ]
    for fetch in fetches:
        fetch.start()

    own_first = core_ref[0] == 0
    rows_half = own_ref.shape[0]
    for index, (i, j) in enumerate(PAIRS):
        at = (index * BLOCK) % rows_half
        own = own_ref[at : at + BLOCK, :]
        other = other_ref[at : at + BLOCK, :]
        block = jnp.where(own_first == (index * BLOCK < rows_half), own, other)
        for part, values in enumerate(split_three(block)):
            gram_ref[part, BLOCK * i : BLOCK * (i + 1), BLOCK * j : BLOCK * (j + 1)] = values
            if i != j:
                gram_ref[part, BLOCK * j : BLOCK * (j + 1), BLOCK * i : BLOCK * (i + 1)] = values.T

    def keep(ref, values, at=0):
        for part, piece in enumerate(split_three(values)):
            ref[RANK * part : RANK * (part + 1), at : at + values.shape[1]] = piece

    def times_gram(at, size):
        span = pl.ds(at, size)
        by_high = dot(image_ref[...], gram_ref[0, :, span], nn)
        by_middle = dot(image_ref[: 2 * RANK, :], gram_ref[1, :, span], nn)
        by_low = dot(image_ref[:RANK, :], gram_ref[2, :, span], nn)
        small = by_middle[RANK:] + (by_high[2 * RANK :] + by_low)
        return by_high[:RANK] + (by_high[RANK : 2 * RANK] + by_middle[:RANK] + small)

    def products():
        total = 0.0
        for at in (0, 256):
            image = image_ref[:, at : at + 256]
            both = dot(image, image[: 2 * RANK], nt)
            small = both[2 * RANK :, :RANK] + dot(image[:RANK], image[2 * RANK :], nt)
            middle = both[:RANK, RANK:] + both[RANK : 2 * RANK, :RANK]
            total = total + (both[:RANK, :RANK] + (middle + (both[RANK : 2 * RANK, RANK:] + small)))
        return total

    def times_inverse(inverse, ref, span=slice(0, N1)):
        high, middle, low = split_three(inverse)
        left = jnp.concatenate([high, low, middle, middle, high, high], axis=1)
        by_high, by_middle, by_low = (ref[RANK * part : RANK * (part + 1), span] for part in range(3))
        right = jnp.concatenate([by_low, by_high, by_middle, by_high, by_middle, by_high], axis=0)
        return dot(left, right, nn)

    keep(image_ref, start_ref[...].T)
    keep(image_ref, times_gram(0, N1))

    def sweep(iteration, carry):
        def beside(r):
            if r in (0, 2):
                keep(ahead_ref, times_gram(128 * r, 256), 128 * r)

        inverse = inverse_factor(products(), beside)
        for at in (0, 256):
            keep(image_ref, times_inverse(inverse, ahead_ref, slice(at, at + 256)), at)
        return carry

    lax.fori_loop(0, ITERS - 1, sweep, 0)

    for fetch in fetches:
        fetch.wait()

    def beside(r):
        if r < len(pieces):
            high_ref[r], low_ref[r] = split(parts_ref[r])

    inverse = inverse_factor(products(), beside)
    basis = times_inverse(inverse, image_ref)
    result_ref[...] = basis.T
    basis_send = pltpu.make_async_copy(result_ref, basis_ref, basis_sent)
    basis_send.start()
    basis_high, basis_low = split(basis)
    basis_parts = jnp.concatenate([basis_high, basis_low], axis=0)
    sends = [
        pltpu.make_async_copy(results_ref.at[c], core_out_ref.at[v, :, span], sent.at[c])
        for c, (v, span) in enumerate(pieces)
    ]
    for c in range(len(pieces)):
        by_high = dot(basis_parts, high_ref[c], nn)
        results_ref[c] = by_high[:RANK] + (by_high[RANK:] + dot(basis_high, low_ref[c], nn))
        sends[c].start()
    basis_send.wait()
    for send in sends:
        send.wait()


def sweeps(core, own, other, start_basis, field):
    variables, _, columns = field.shape
    parts = variables * columns // STEP
    whole = pl.BlockSpec(memory_space=pltpu.VMEM)
    anywhere = pl.BlockSpec(memory_space=pltpu.HBM)
    return pl.pallas_call(
        sweeps_kernel,
        in_specs=[pl.BlockSpec(memory_space=pltpu.SMEM), whole, whole, whole, anywhere],
        out_specs=[anywhere, anywhere],
        out_shape=[
            jax.ShapeDtypeStruct((variables, RANK, columns), jnp.float32),
            jax.ShapeDtypeStruct((N1, RANK), jnp.float32),
        ],
        scratch_shapes=[
            pltpu.VMEM((3, N1, N1), jnp.bfloat16),
            pltpu.VMEM((3 * RANK, N1), jnp.bfloat16),
            pltpu.VMEM((3 * RANK, N1), jnp.bfloat16),
            pltpu.VMEM((parts, N1, STEP), jnp.float32),
            pltpu.VMEM((parts, N1, STEP), jnp.bfloat16),
            pltpu.VMEM((parts, N1, STEP), jnp.bfloat16),
            pltpu.VMEM((parts, RANK, STEP), jnp.float32),
            pltpu.VMEM((N1, RANK), jnp.float32),
            pltpu.SemaphoreType.DMA((parts,)),
            pltpu.SemaphoreType.DMA((parts,)),
            pltpu.SemaphoreType.DMA,
        ],
        compiler_params=pltpu.CompilerParams(vmem_limit_bytes=51 << 20),
    )(core, own, other, start_basis, field)


def spread(block, axes, size):
    return lax.all_to_all(jnp.broadcast_to(block, (size,) + block.shape), axes, 0, 0)


def all_sum(packed):
    core = lax.axis_index("core")
    half = packed.shape[0] // 2
    swap = [(0, 1), (1, 0)]
    mine = lax.dynamic_slice_in_dim(packed, core * half, half)
    theirs = lax.dynamic_slice_in_dim(packed, (1 - core) * half, half)
    own = mine + lax.ppermute(theirs, "core", swap)
    plane = lax.axis_size("y") * lax.axis_size("x")
    piece = half // plane
    pieces = lax.all_to_all(own.reshape(plane, piece, BLOCK), ("y", "x"), 0, 0)
    own = jnp.sum(pieces, axis=0)
    for flip in (1, 2, 7):
        own = own + lax.ppermute(own, "z", [(i, i ^ flip) for i in range(lax.axis_size("z"))])
    own = spread(own, ("y", "x"), plane).reshape(half, BLOCK)
    return core, own, lax.ppermute(own, "core", swap)


def local(tensor_field, start_basis):
    packed = partial_gram(tensor_field).reshape(len(PAIRS) * BLOCK, BLOCK)
    core, own, other = all_sum(packed)
    return tuple(sweeps(core.astype(jnp.int32).reshape(1), own, other, start_basis, tensor_field))


def solution(mesh):
    fine = Mesh(mesh.devices.reshape(8, 4, 4, 2), ("z", "y", "x", "core"))
    spec = P(("x", "core"), None, ("z", "y"))
    return jax.shard_map(local, mesh=fine, in_specs=(spec, P()), out_specs=(spec, P()), check_vma=False)
```
